32 devices in a mesh: wide: 8 (over z, x), narrow: 4 (over y, core).
Axes of the slice: x: 2, y: 2, z: 4, core: 2. Of those that a mesh axis runs over, the one named last changes fastest.
Arguments:
- grid_adjoint_fields: bfloat16 [64, 2560, 512], P('wide', 'narrow'), may hold values from -6 to 6
- interp_weights: bfloat16 [5120, 32, 32], P(('wide', 'narrow')), may hold values from -1 to 1
- depart_owner: int32 [5120, 1], P(('wide', 'narrow')), may hold values from 0 to 7; in each aligned block of 160 rows (0 to 159, 160 to 319, ...) at most 40 rows name the same one
- depart_block: int32 [5120], P(('wide', 'narrow')), may hold values from 0 to 159
- wave_perm: int32 [512], replicated, may hold values from 0 to 511, each once
- legendre: bfloat16 [512, 64, 512], P(('wide', 'narrow')), may hold values from -0.75 to 0.75
- mode_proj: float32 [512, 512], replicated, may hold values from -0.25 to 0.25
- mode_back: float32 [512, 512], replicated, may hold values from -0.25 to 0.25
- mode_depth: float32 [512], replicated, may hold values from 1e-06 to 0.001
Outputs:
- adj_out: float32 [64, 2560, 512], P('wide', 'narrow')
The draws below stay inside these ranges and needn't reach their ends.
Inputs may be any that keep to these rules, and one draw needn't show every extreme that they name: `depart_owner`: each block's departure owner shares the block's narrow index. Among the 160 blocks of one device at most 40 name one owner, and exactly 40 do in some devices. `wave_perm`: every wavenumber appears once.
All inputs are finite; a program needn't handle non-finite values.
Results may differ from the reference program's by a relative error of at most 0.013.
Values may be sent and summed in bfloat16 or wider, within the bound.
A program may use at most 256 MiB of HBM per device.

```python
import math
import jax
import jax.numpy as jnp
import numpy as np
from jax import lax

NLON = 2560
M = 512
LAT_DEV = 8
BS = 32
C = 512
NLAT = 64
LON_DEV = 640
NB_DEV = 160
NBLOCKS = 5120
CAP = 40
N_WIDE = 8
N_NARROW = 4


def plant(result, stream_key, low, top_value):
    place = [jax.random.randint(jax.random.fold_in(stream_key, axis), (), 0, length) for axis, length in enumerate(result.shape)]
    widest = result.shape.index(max(result.shape))
    neighbour = place[:widest] + [(place[widest] + 1) % result.shape[widest]] + place[widest + 1:]
    return result.at[tuple(place)].set(low).at[tuple(neighbour)].set(top_value)


def shard_levels(stream_key, shape, cuts, low, top_value):
    factor_of, own = 1.0, jax.random.fold_in(stream_key, 6)
    for position, blocks in cuts:
        draws = jnp.exp(jax.random.uniform(jax.random.fold_in(own, position), (blocks,), jnp.float32, low / len(cuts), top_value / len(cuts)))
        factor_of = factor_of * jnp.repeat(draws, shape[position] // blocks).reshape([-1 if axis == position else 1 for axis in range(len(shape))])
    return factor_of


def deal_out(key, own, number, rows, count, top, limit, skew):
    order = jax.random.permutation(key, count)
    crowded, common = portions_of(count, rows * top, limit, skew, True), portions_of(count, rows * top, limit, skew, False)
    places = jnp.arange(count)

    def named(lengths, rotation):
        used = int((lengths > 0).sum())
        fixed = max(1, used // 4)
        shifted = fixed + (places - fixed + rotation * (used - fixed)) % max(1, count - fixed)
        return jnp.zeros((count,), jnp.int32).at[order[jnp.where(places < fixed, places, shifted)]].set(jnp.asarray(lengths, jnp.int32))

    lengths = jnp.where(number % 4 == 0, named(crowded, number // 4), named(common, number - number // 4 - 1))
    mixed = jax.random.permutation(jax.random.fold_in(own, 3), count)
    donor, taker = mixed[0:count // 2 * 2:2], mixed[1:count // 2 * 2:2]
    room = jnp.minimum(lengths[donor] - 1, limit - lengths[taker]) // 2
    room = jnp.where((donor == order[0]) | (taker == order[0]) | (lengths[taker] == 0), 0, jnp.maximum(room, 0))
    shifted = jax.random.randint(jax.random.fold_in(own, 4), (count // 2,), 0, 1 << 20) % (room + 1)
    lengths = lengths.at[donor].add(-shifted).at[taker].add(shifted)
    members = jnp.searchsorted(jnp.cumsum(lengths), jnp.arange(rows * top), side="right").astype(jnp.int32)
    grid = members.reshape(top, rows).T
    grid = grid[jax.random.permutation(jax.random.fold_in(own, 1), rows)]
    rotation = jax.random.randint(jax.random.fold_in(own, 2), (rows, 1), 0, top)
    return jnp.take_along_axis(grid, (jnp.arange(top)[None, :] + rotation) % top, axis=1)


def portions_of(amount, total, most, skew, full):
    portions = [(1 << 20) // math.isqrt(rank ** skew) + 1 for rank in range(1, amount + 1)]
    largest = most if full else min(most, max(-(-total // amount), total * portions[0] // sum(portions)))
    least = 1 if total - largest >= amount - 1 else 0
    holding, rest = [largest] + [least] * (amount - 1), total - largest - least * (amount - 1)
    while rest > 0:
        free = [i for i in range(1, amount) if holding[i] < largest] or [i for i in range(1, amount) if holding[i] < most]
        whole, budget = sum([portions[i] for i in free]), rest
        for i in free:
            more = min(most - holding[i], max(1, budget * portions[i] // whole), rest)
            holding[i] = holding[i] + more
            rest = rest - more
    return np.array(holding)


def centred(stream_key, extent, deviation, bound, cuts=(), kind=jnp.bfloat16):
    entries = deviation * jax.random.normal(stream_key, extent, jnp.float32)
    if cuts:
        entries = entries * shard_levels(stream_key, extent, cuts, -0.22, 0.18)
    return jnp.clip(entries, -bound, bound).astype(kind)


def setup_inputs(seed: int = 0) -> dict:
    streams_of = jax.random.split(jax.random.key(seed), 10)
    grid_adjoint_fields = centred(streams_of[0], (NLAT, NLON, C), 1.0, 6.0, ((0, 8), (1, 4)))
    interp_weights = centred(streams_of[1], (NBLOCKS, BS, BS), BS ** -0.5, 1.0, ((0, 32),))
    depart_owner_keys = jax.random.split(jax.random.fold_in(streams_of[2], 1), NBLOCKS // NB_DEV)
    depart_owner_turns = jax.random.permutation(jax.random.fold_in(streams_of[2], 3), NBLOCKS // NB_DEV)
    depart_owner = jax.vmap(lambda own, number: deal_out(jax.random.fold_in(streams_of[2], 2), own, number, NB_DEV, N_WIDE, 1, CAP, 2))(depart_owner_keys, depart_owner_turns).reshape((NBLOCKS, 1))
    depart_block = plant(jax.random.randint(streams_of[3], (NBLOCKS,), 0, NB_DEV), jax.random.fold_in(streams_of[3], 1), 0, NB_DEV - 1).astype(jnp.int32)
    wave_perm = jax.random.permutation(streams_of[4], M).astype(jnp.int32)
    legendre = centred(streams_of[5], (M, NLAT, M), NLAT ** -0.5, 0.75, ((0, 32),))
    mode_proj = centred(streams_of[6], (C, C), C ** -0.5, 0.25, (), jnp.float32)
    mode_back = centred(streams_of[7], (C, C), C ** -0.5, 0.25, (), jnp.float32)
    mode_depth = jnp.clip(jnp.exp(jax.random.uniform(streams_of[8], (C,), jnp.float32, math.log(9.999999974752427e-07), math.log(0.001))), 9.999999974752427e-07, 0.001)
    return dict(grid_adjoint_fields=grid_adjoint_fields, interp_weights=interp_weights, depart_owner=depart_owner, depart_block=depart_block, wave_perm=wave_perm, legendre=legendre, mode_proj=mode_proj, mode_back=mode_back, mode_depth=mode_depth)


def trig_table(lon_index, col_index, wave_perm):
    wavenumber = jnp.take(wave_perm, col_index // 2)
    phase_int = (lon_index[:, None] * wavenumber[None, :]) % NLON
    angles = phase_int.astype(jnp.float32) * (2.0 * math.pi / NLON)
    values = jnp.where((col_index % 2 == 0)[None, :], jnp.cos(angles), jnp.sin(angles))
    return values.astype(jnp.bfloat16)


def apply_modes(spectra, mode_proj, mode_back, mode_depth):
    slot_count, degrees, parts, channels = spectra.shape
    mode_rows = jnp.dot(spectra.reshape(-1, channels), mode_proj, precision=lax.Precision.HIGHEST, preferred_element_type=jnp.float32)
    degree_float = jnp.arange(degrees, dtype=jnp.float32)
    damping = 1.0 / (1.0 + (degree_float * (degree_float + 1.0))[:, None] * mode_depth[None, :])
    mode_rows = mode_rows.reshape(slot_count, degrees, parts, channels) * damping[None, :, None, :]
    returned = jnp.dot(mode_rows.reshape(-1, channels), mode_back, precision=lax.Precision.HIGHEST, preferred_element_type=jnp.float32)
    return returned.astype(jnp.bfloat16).reshape(slot_count, degrees, parts, channels)


def reference(grid_adjoint_fields, interp_weights, depart_owner, depart_block, wave_perm, legendre, mode_proj, mode_back, mode_depth):
    normalizing_scale = NLON ** -0.5
    trig_rows = trig_table(jnp.arange(NLON, dtype=jnp.int32), jnp.arange(2 * M, dtype=jnp.int32), wave_perm)
    trigonometric_floats = trig_rows.astype(jnp.float32)
    fourier_harmonics = (jnp.einsum('brw,rk->bkw', grid_adjoint_fields.astype(jnp.float32), trigonometric_floats) * normalizing_scale).astype(jnp.bfloat16)
    degree = jnp.arange(M, dtype=jnp.int32)
    keep_mask = degree[None, None, :] >= wave_perm[:, None, None]
    masked_values = jnp.where(keep_mask, legendre, jnp.zeros_like(legendre)).astype(jnp.float32)
    fourier_sets = fourier_harmonics.reshape(NLAT, M, 2, C).astype(jnp.float32)
    spectra = jnp.einsum('jgn,gjpc->jnpc', masked_values, fourier_sets)
    returned = apply_modes(spectra, mode_proj, mode_back, mode_depth)
    synthesis_output = jnp.einsum('jgn,jnpc->gjpc', masked_values, returned.astype(jnp.float32)).astype(jnp.bfloat16)
    synthesis_output = synthesis_output.reshape(NLAT, 2 * M, C)
    wavenumber_grid = (jnp.einsum('yzw,rz->yrw', synthesis_output.astype(jnp.float32), trigonometric_floats) * normalizing_scale).astype(jnp.bfloat16)
    blocks_per_row = LON_DEV // BS
    blocks = grid_adjoint_fields.reshape(N_WIDE, LAT_DEV, N_NARROW, blocks_per_row, BS, C).transpose(0, 2, 1, 3, 4, 5).reshape(NBLOCKS, BS, C)
    contrib = jnp.einsum('bai,bac->bic', interp_weights.astype(jnp.float32), blocks.astype(jnp.float32)).astype(jnp.bfloat16)
    source = jnp.arange(NBLOCKS, dtype=jnp.int32)
    narrow_of = (source // NB_DEV) % N_NARROW
    target = (depart_owner[:, 0] * N_NARROW + narrow_of) * NB_DEV + depart_block
    deposit = jax.ops.segment_sum(contrib.astype(jnp.float32), target, num_segments=NBLOCKS)
    deposit_grid = deposit.reshape(N_WIDE, N_NARROW, LAT_DEV, blocks_per_row, BS, C).transpose(0, 2, 1, 3, 4, 5).reshape(NLAT, NLON, C)
    return wavenumber_grid.astype(jnp.float32) + deposit_grid
```

```python
import math

import jax
import jax.numpy as jnp
from jax import lax
from jax.experimental import pallas as pl
from jax.experimental.pallas import tpu as pltpu
from jax.sharding import PartitionSpec as P

NLON = 2560
BS = 32
VMEM_LIMIT = 48 * 1024 * 1024
SCALE = NLON ** (-0.5)


def params():
    return pltpu.CompilerParams(vmem_limit_bytes=VMEM_LIMIT)


def cost(flops, nbytes):
    return pl.CostEstimate(flops=flops, bytes_accessed=nbytes, transcendentals=0)


def trig_tables(first_lon, lon_dev, wavenumber):
    columns = 2 * wavenumber.shape[0]
    wave = jnp.broadcast_to(wavenumber[:, None], (wavenumber.shape[0], 2)).reshape(columns)
    shift = (jnp.arange(columns, dtype=jnp.int32) % 2) * (NLON - NLON // 4)
    unit = 2.0 * math.pi / NLON
    coarse_lon = first_lon + BS * jnp.arange(lon_dev // BS, dtype=jnp.int32)
    coarse = ((coarse_lon[:, None] * wave[None, :] + shift[None, :]) % NLON).astype(jnp.float32) * unit
    fine_lon = jnp.arange(BS, dtype=jnp.int32)
    fine = ((fine_lon[:, None] * wave[None, :]) % NLON).astype(jnp.float32) * unit
    parts = lax.optimization_barrier((jnp.cos(coarse), jnp.sin(coarse), jnp.cos(fine), jnp.sin(fine)))
    cos_a, sin_a, cos_b, sin_b = parts
    table = cos_a[:, None, :] * cos_b[None, :, :] - sin_a[:, None, :] * sin_b[None, :, :]
    return table.astype(jnp.bfloat16).reshape(lon_dev, columns)


def analysis_body(trig_ref, grid_ref, out_ref):
    out_ref[0] = jnp.dot(
        trig_ref[...], grid_ref[0], preferred_element_type=jnp.float32
    ).astype(jnp.bfloat16)


def analysis(trig_t, grid):
    lat_dev, lon_dev, channels = grid.shape
    columns = trig_t.shape[0]
    return pl.pallas_call(
        analysis_body,
        grid=(lat_dev,),
        in_specs=[
            pl.BlockSpec((columns, lon_dev), lambda a: (0, 0)),
            pl.BlockSpec((1, lon_dev, channels), lambda a: (a, 0, 0)),
        ],
        out_specs=pl.BlockSpec((1, columns, channels), lambda a: (a, 0, 0)),
        out_shape=jax.ShapeDtypeStruct((lat_dev, columns, channels), jnp.bfloat16),
        compiler_params=params(),
        cost_estimate=cost(
            2 * columns * lon_dev * lat_dev * channels,
            2 * (lat_dev * (columns + lon_dev) * channels + columns * lon_dev),
        ),
        name="analysis",
    )(trig_t, grid)


def modes_body(wave_ref, legendre_ref, fourier_ref, proj_ref, back_ref, damping_ref, out_ref):
    slot = pl.program_id(0)
    bands, parts, lat_dev, channels = fourier_ref.shape
    lats = bands * lat_dev
    degrees = legendre_ref.shape[2]
    degree = lax.broadcasted_iota(jnp.int32, (lats, degrees), 1)
    masked = jnp.where(
        degree >= wave_ref[slot], legendre_ref[0].astype(jnp.float32), 0.0
    ).astype(jnp.bfloat16)
    fourier = fourier_ref[...].astype(jnp.float32)
    rows = jnp.concatenate(
        [fourier[:, p].reshape(lats, channels) for p in range(parts)], axis=0
    ).astype(jnp.bfloat16)
    projected = jnp.dot(rows, proj_ref[...], preferred_element_type=jnp.float32) * SCALE
    projected = projected.astype(jnp.bfloat16)
    sums = []
    for p in range(parts):
        modal = lax.dot_general(
            masked,
            projected[p * lats : (p + 1) * lats],
            (((0,), (0,)), ((), ())),
            preferred_element_type=jnp.float32,
        )
        modal = (modal * damping_ref[...]).astype(jnp.bfloat16)
        sums.append(jnp.dot(masked, modal, preferred_element_type=jnp.float32))
    back = jnp.dot(
        jnp.concatenate(sums, axis=0).astype(jnp.bfloat16),
        back_ref[...],
        preferred_element_type=jnp.float32,
    )
    for p in range(parts):
        out_ref[:, p] = (
            back[p * lats : (p + 1) * lats].reshape(bands, lat_dev, channels).astype(jnp.bfloat16)
        )


def modes(wavenumber, legendre, fourier, proj, back, damping):
    slots, lats, degrees = legendre.shape
    bands, _, lat_dev, channels = fourier.shape
    spec = pl.BlockSpec((bands, 2, lat_dev, channels), lambda j, w: (0, j, 0, 0))
    whole = lambda j, w: (0, 0)
    return pl.pallas_call(
        modes_body,
        grid_spec=pltpu.PrefetchScalarGridSpec(
            num_scalar_prefetch=1,
            grid=(slots,),
            in_specs=[
                pl.BlockSpec((1, lats, degrees), lambda j, w: (j, 0, 0)),
                spec,
                pl.BlockSpec(proj.shape, whole),
                pl.BlockSpec(back.shape, whole),
                pl.BlockSpec(damping.shape, whole),
            ],
            out_specs=spec,
        ),
        out_shape=jax.ShapeDtypeStruct(fourier.shape, jnp.bfloat16),
        compiler_params=params(),
        cost_estimate=cost(
            slots * 2 * 4 * 2 * lats * channels * degrees,
            2 * (2 * fourier.size + legendre.size) + 8 * proj.size,
        ),
        name="modes",
    )(wavenumber, legendre, fourier, proj, back, damping)


def pack_body(source_ref, contrib_ref, out_ref):
    def step(s, carry):
        out_ref[s] = contrib_ref[source_ref[s]]
        return carry

    lax.fori_loop(0, out_ref.shape[0], step, 0, unroll=4)


def pack(source, contrib):
    count = source.shape[0]
    shape = (count,) + contrib.shape[1:]
    return pl.pallas_call(
        pack_body,
        grid_spec=pltpu.PrefetchScalarGridSpec(
            num_scalar_prefetch=1,
            grid=(1,),
            in_specs=[pl.BlockSpec(contrib.shape, lambda i, s: (0, 0, 0))],
            out_specs=pl.BlockSpec(shape, lambda i, s: (0, 0, 0)),
        ),
        out_shape=jax.ShapeDtypeStruct(shape, jnp.bfloat16),
        compiler_params=params(),
        cost_estimate=cost(math.prod(shape), 4 * math.prod(shape)),
        name="pack",
    )(source, contrib)


def deposit_body(target_ref, values_ref, out_ref):
    out_ref[...] = jnp.zeros_like(out_ref)

    def step(s, carry):
        block = target_ref[s]

        @pl.when(block >= 0)
        def _():
            out_ref[block] += values_ref[s].astype(jnp.float32)

        return carry

    lax.fori_loop(0, values_ref.shape[0], step, 0, unroll=4)


def deposit(target, values, block_count):
    shape = (block_count,) + values.shape[1:]
    return pl.pallas_call(
        deposit_body,
        grid_spec=pltpu.PrefetchScalarGridSpec(
            num_scalar_prefetch=1,
            grid=(1,),
            in_specs=[pl.BlockSpec(values.shape, lambda i, s: (0, 0, 0))],
            out_specs=pl.BlockSpec(shape, lambda i, s: (0, 0, 0)),
        ),
        out_shape=jax.ShapeDtypeStruct(shape, jnp.float32),
        compiler_params=params(),
        cost_estimate=cost(values.size, 2 * values.size + 4 * math.prod(shape)),
        name="deposit",
    )(target, values)


def synthesis_body(trig_ref, rows_ref, *refs):
    deposits, out_ref = refs[:-1], refs[-1]
    sets, _, per_set, channels = rows_ref.shape
    rows = rows_ref[...].reshape(sets * per_set, channels)
    wave = jnp.dot(trig_ref[...], rows, preferred_element_type=jnp.float32) * SCALE
    wave = wave.astype(jnp.bfloat16).astype(jnp.float32).reshape(out_ref.shape[1:])
    start = 0
    for part in deposits:
        stop = start + part.shape[1]
        out_ref[0, :, start:stop] = wave[:, start:stop] + part[...]
        start = stop


def synthesis(trig, rows, deposits, lat_dev, blocks_per_row):
    sets, _, per_set, channels = rows.shape
    return pl.pallas_call(
        synthesis_body,
        grid=(lat_dev,),
        in_specs=[
            pl.BlockSpec(trig.shape, lambda a: (0, 0)),
            pl.BlockSpec((sets, 1, per_set, channels), lambda a: (0, a, 0, 0)),
        ]
        + [
            pl.BlockSpec((blocks_per_row,) + part.shape[1:], lambda a: (a, 0, 0))
            for part in deposits
        ],
        out_specs=pl.BlockSpec((1, blocks_per_row, BS, channels), lambda a: (a, 0, 0, 0)),
        out_shape=jax.ShapeDtypeStruct((lat_dev, blocks_per_row, BS, channels), jnp.float32),
        compiler_params=params(),
        cost_estimate=cost(
            2 * trig.size * lat_dev * channels,
            2 * (trig.size + rows.size) + 8 * lat_dev * trig.shape[0] * channels,
        ),
        name="synthesis",
    )(trig, rows, *deposits)


def shards(
    grid_adjoint_fields,
    interp_weights,
    depart_owner,
    depart_block,
    wave_perm,
    legendre,
    mode_proj,
    mode_back,
    mode_depth,
):
    wide_count = lax.axis_size("wide")
    narrow_count = lax.axis_size("narrow")
    wide_index = lax.axis_index("wide")
    narrow_index = lax.axis_index("narrow")
    lat_dev, lon_dev, channels = grid_adjoint_fields.shape
    slot_count, lat_total, degrees = legendre.shape
    per_set = 2 * degrees // narrow_count
    blocks_per_row = lon_dev // BS
    block_count = lat_dev * blocks_per_row
    split = BS // 2

    owner_band = depart_owner[:, 0]
    block_ids = jnp.arange(block_count, dtype=jnp.int32)
    capacity = (2 * block_count + wide_count - 1) // wide_count
    same_owner = owner_band[:, None] == owner_band[None, :]
    earlier = block_ids[None, :] < block_ids[:, None]
    slot_rank = jnp.sum((same_owner & earlier).astype(jnp.int32), axis=1)
    send_slot = owner_band * capacity + slot_rank
    pick_slot = jnp.arange(wide_count * capacity, dtype=jnp.int32)[:, None] == send_slot[None, :]
    source = jnp.max(jnp.where(pick_slot, block_ids[None, :], 0), axis=1)
    slot_target = jnp.max(jnp.where(pick_slot, depart_block[None, :], -1), axis=1).reshape(
        wide_count, capacity
    )
    recv_targets = lax.all_to_all(
        slot_target, "wide", split_axis=0, concat_axis=0, tiled=True
    ).reshape(-1)
    blocks = grid_adjoint_fields.reshape(block_count, BS, channels)
    contrib = jnp.einsum(
        "bai,bac->bic", interp_weights, blocks, preferred_element_type=jnp.float32
    ).astype(jnp.bfloat16)
    packed = [
        pack(source, contrib[:, :split]).reshape(wide_count, capacity, split, channels),
        pack(source, contrib[:, split:]).reshape(wide_count, capacity, BS - split, channels),
    ]

    def exchange(values):
        return lax.all_to_all(values, "wide", split_axis=0, concat_axis=0, tiled=True)

    wavenumber = wave_perm.reshape(wide_count, narrow_count, slot_count)
    own_wave = lax.dynamic_index_in_dim(
        lax.dynamic_index_in_dim(wavenumber, wide_index, 0, False), narrow_index, 0, False
    )
    order = wavenumber.transpose(1, 0, 2).reshape(-1)
    trig = trig_tables(narrow_index * lon_dev, lon_dev, order)

    first_recv = exchange(packed[0])
    partial = analysis(trig.T, grid_adjoint_fields)
    summed = lax.psum_scatter(
        partial.reshape(lat_dev, narrow_count, per_set, channels),
        "narrow",
        scatter_dimension=1,
        tiled=False,
    )
    summed, first_recv = lax.optimization_barrier((summed, first_recv))
    fourier = exchange(
        summed.reshape(lat_dev, wide_count, 2 * slot_count, channels).transpose(1, 2, 0, 3)
    )
    degree_float = jnp.arange(degrees, dtype=jnp.float32)
    damping = 1.0 / (1.0 + (degree_float * (degree_float + 1.0))[:, None] * mode_depth[None, :])
    synth = modes(
        own_wave,
        legendre,
        fourier,
        mode_proj.astype(jnp.bfloat16),
        mode_back.astype(jnp.bfloat16),
        damping,
    )
    synth = exchange(synth)
    synth, second = lax.optimization_barrier((synth, packed[1]))
    second_recv = exchange(second)
    rows = lax.all_gather(
        synth.reshape(per_set, lat_dev, channels).transpose(1, 0, 2), "narrow", axis=0, tiled=False
    )
    deposits = [
        deposit(recv_targets, recv.reshape(wide_count * capacity, -1, channels), block_count)
        for recv in (first_recv, second_recv)
    ]
    out = synthesis(trig, rows, deposits, lat_dev, blocks_per_row)
    return out.reshape(lat_dev, lon_dev, channels)


def solution(mesh):
    in_specs = (
        P("wide", "narrow", None),
        P(("wide", "narrow"), None, None),
        P(("wide", "narrow"), None),
        P(("wide", "narrow")),
        P(),
        P(("wide", "narrow"), None, None),
        P(),
        P(),
        P(),
    )
    out_specs = P("wide", "narrow", None)
    return jax.shard_map(shards, mesh=mesh, in_specs=in_specs, out_specs=out_specs, check_vma=False)
```

```python
import math

import jax
import jax.numpy as jnp
from jax import lax
from jax.experimental import pallas as pl
from jax.experimental.pallas import tpu as pltpu
from jax.sharding import PartitionSpec as P

NLON = 2560
BS = 32
VMEM_LIMIT = 48 * 1024 * 1024
SCALE = NLON ** (-0.5)


def params():
    return pltpu.CompilerParams(vmem_limit_bytes=VMEM_LIMIT)


def cost(flops, nbytes):
    return pl.CostEstimate(flops=flops, bytes_accessed=nbytes, transcendentals=0)


def trig_tables(first_lon, lon_dev, wavenumber):
    columns = 2 * wavenumber.shape[0]
    wave = jnp.broadcast_to(wavenumber[:, None], (wavenumber.shape[0], 2)).reshape(columns)
    shift = (jnp.arange(columns, dtype=jnp.int32) % 2) * (NLON - NLON // 4)
    unit = 2.0 * math.pi / NLON
    coarse_lon = first_lon + BS * jnp.arange(lon_dev // BS, dtype=jnp.int32)
    coarse = ((coarse_lon[:, None] * wave[None, :] + shift[None, :]) % NLON).astype(jnp.float32) * unit
    fine_lon = jnp.arange(BS, dtype=jnp.int32)
    fine = ((fine_lon[:, None] * wave[None, :]) % NLON).astype(jnp.float32) * unit
    parts = lax.optimization_barrier((jnp.cos(coarse), jnp.sin(coarse), jnp.cos(fine), jnp.sin(fine)))
    cos_a, sin_a, cos_b, sin_b = parts
    table = cos_a[:, None, :] * cos_b[None, :, :] - sin_a[:, None, :] * sin_b[None, :, :]
    return table.astype(jnp.bfloat16).reshape(lon_dev, columns)


def analysis_body(trig_ref, grid_ref, out_ref):
    rows = jnp.dot(trig_ref[...], grid_ref[0], preferred_element_type=jnp.float32)
    out_ref[...] = rows.astype(jnp.bfloat16).reshape(out_ref.shape)


def analysis(trig_t, grid, sets):
    lat_dev, lon_dev, channels = grid.shape
    columns = trig_t.shape[0]
    per_set = columns // sets
    return pl.pallas_call(
        analysis_body,
        grid=(lat_dev,),
        in_specs=[
            pl.BlockSpec((columns, lon_dev), lambda a: (0, 0)),
            pl.BlockSpec((1, lon_dev, channels), lambda a: (a, 0, 0)),
        ],
        out_specs=pl.BlockSpec((sets, 1, per_set, channels), lambda a: (0, a, 0, 0)),
        out_shape=jax.ShapeDtypeStruct((sets, lat_dev, per_set, channels), jnp.bfloat16),
        compiler_params=params(),
        cost_estimate=cost(
            2 * columns * lon_dev * lat_dev * channels,
            2 * (lat_dev * (columns + lon_dev) * channels + columns * lon_dev),
        ),
        name="analysis",
    )(trig_t, grid)


def modes_body(wave_ref, legendre_ref, fourier_ref, proj_ref, back_ref, damping_ref, out_ref):
    slot = pl.program_id(0)
    bands, parts, lat_dev, channels = fourier_ref.shape
    lats = bands * lat_dev
    degrees = legendre_ref.shape[2]
    degree = lax.broadcasted_iota(jnp.int32, (lats, degrees), 1)
    masked = jnp.where(
        degree >= wave_ref[slot], legendre_ref[0].astype(jnp.float32), 0.0
    ).astype(jnp.bfloat16)
    fourier = fourier_ref[...].astype(jnp.float32)
    rows = jnp.concatenate(
        [fourier[:, p].reshape(lats, channels) for p in range(parts)], axis=0
    ).astype(jnp.bfloat16)
    projected = jnp.dot(rows, proj_ref[...], preferred_element_type=jnp.float32) * SCALE
    projected = projected.astype(jnp.bfloat16)
    sums = []
    for p in range(parts):
        modal = lax.dot_general(
            masked,
            projected[p * lats : (p + 1) * lats],
            (((0,), (0,)), ((), ())),
            preferred_element_type=jnp.float32,
        )
        modal = (modal * damping_ref[...]).astype(jnp.bfloat16)
        sums.append(jnp.dot(masked, modal, preferred_element_type=jnp.float32))
    back = jnp.dot(
        jnp.concatenate(sums, axis=0).astype(jnp.bfloat16),
        back_ref[...],
        preferred_element_type=jnp.float32,
    )
    for p in range(parts):
        out_ref[:, p] = (
            back[p * lats : (p + 1) * lats].reshape(bands, lat_dev, channels).astype(jnp.bfloat16)
        )


def modes(wavenumber, legendre, fourier, proj, back, damping):
    slots, lats, degrees = legendre.shape
    bands, _, lat_dev, channels = fourier.shape
    spec = pl.BlockSpec((bands, 2, lat_dev, channels), lambda j, w: (0, j, 0, 0))
    whole = lambda j, w: (0, 0)
    return pl.pallas_call(
        modes_body,
        grid_spec=pltpu.PrefetchScalarGridSpec(
            num_scalar_prefetch=1,
            grid=(slots,),
            in_specs=[
                pl.BlockSpec((1, lats, degrees), lambda j, w: (j, 0, 0)),
                spec,
                pl.BlockSpec(proj.shape, whole),
                pl.BlockSpec(back.shape, whole),
                pl.BlockSpec(damping.shape, whole),
            ],
            out_specs=spec,
        ),
        out_shape=jax.ShapeDtypeStruct(fourier.shape, jnp.bfloat16),
        compiler_params=params(),
        cost_estimate=cost(
            slots * 2 * 4 * 2 * lats * channels * degrees,
            2 * (2 * fourier.size + legendre.size) + 8 * proj.size,
        ),
        name="modes",
    )(wavenumber, legendre, fourier, proj, back, damping)


def pack_body(source_ref, contrib_ref, out_ref):
    def step(s, carry):
        out_ref[s] = contrib_ref[source_ref[s]]
        return carry

    lax.fori_loop(0, out_ref.shape[0], step, 0, unroll=4)


def pack(source, contrib, half):
    count = source.shape[0]
    blocks, cells, channels = contrib.shape
    shape = (count, cells // 2, channels)
    return pl.pallas_call(
        pack_body,
        grid_spec=pltpu.PrefetchScalarGridSpec(
            num_scalar_prefetch=1,
            grid=(1,),
            in_specs=[pl.BlockSpec((blocks, cells // 2, channels), lambda i, s: (0, half, 0))],
            out_specs=pl.BlockSpec(shape, lambda i, s: (0, 0, 0)),
        ),
        out_shape=jax.ShapeDtypeStruct(shape, jnp.bfloat16),
        compiler_params=params(),
        cost_estimate=cost(math.prod(shape), 4 * math.prod(shape)),
        name="pack",
    )(source, contrib)


def deposit_body(target_ref, values_ref, out_ref):
    out_ref[...] = jnp.zeros_like(out_ref)

    def step(s, carry):
        block = target_ref[s]

        @pl.when(block >= 0)
        def _():
            out_ref[block] += values_ref[s].astype(jnp.float32)

        return carry

    lax.fori_loop(0, values_ref.shape[0], step, 0, unroll=4)


def deposit(target, values, block_count):
    shape = (block_count,) + values.shape[1:]
    return pl.pallas_call(
        deposit_body,
        grid_spec=pltpu.PrefetchScalarGridSpec(
            num_scalar_prefetch=1,
            grid=(1,),
            in_specs=[pl.BlockSpec(values.shape, lambda i, s: (0, 0, 0))],
            out_specs=pl.BlockSpec(shape, lambda i, s: (0, 0, 0)),
        ),
        out_shape=jax.ShapeDtypeStruct(shape, jnp.float32),
        compiler_params=params(),
        cost_estimate=cost(values.size, 2 * values.size + 4 * math.prod(shape)),
        name="deposit",
    )(target, values)


def synthesis_body(trig_ref, rows_ref, first_ref, out_ref):
    sets, _, per_set, channels = rows_ref.shape
    half = first_ref.shape[1]
    rows = rows_ref[...].reshape(sets * per_set, channels)
    wave = jnp.dot(trig_ref[...], rows, preferred_element_type=jnp.float32) * SCALE
    wave = wave.astype(jnp.bfloat16).astype(jnp.float32).reshape(out_ref.shape)
    out_ref[:, :half] = wave[:, :half] + first_ref[...]
    out_ref[:, half:] = wave[:, half:]


def synthesis(trig, rows, first):
    sets, lat_dev, per_set, channels = rows.shape
    block_count, half, _ = first.shape
    per_row = block_count // lat_dev
    return pl.pallas_call(
        synthesis_body,
        grid=(lat_dev,),
        in_specs=[
            pl.BlockSpec(trig.shape, lambda a: (0, 0)),
            pl.BlockSpec((sets, 1, per_set, channels), lambda a: (0, a, 0, 0)),
            pl.BlockSpec((per_row, half, channels), lambda a: (a, 0, 0)),
        ],
        out_specs=pl.BlockSpec((per_row, BS, channels), lambda a: (a, 0, 0)),
        out_shape=jax.ShapeDtypeStruct((block_count, BS, channels), jnp.float32),
        compiler_params=params(),
        cost_estimate=cost(
            2 * trig.size * lat_dev * channels,
            2 * (trig.size + rows.size) + 6 * lat_dev * trig.shape[0] * channels,
        ),
        name="synthesis",
    )(trig, rows, first)


def finish_body(target_ref, values_ref, base_ref, out_ref):
    out_ref[...] = base_ref[...]

    def step(s, carry):
        block = target_ref[s]

        @pl.when(block >= 0)
        def _():
            out_ref[block] += values_ref[s].astype(jnp.float32)

        return carry

    lax.fori_loop(0, values_ref.shape[0], step, 0, unroll=4)


def finish(target, values, base):
    count, half, channels = values.shape
    block_count = base.shape[0]
    width = channels // 2
    spec = pl.BlockSpec((block_count, half, width), lambda i, s: (0, 1, i))
    return pl.pallas_call(
        finish_body,
        grid_spec=pltpu.PrefetchScalarGridSpec(
            num_scalar_prefetch=1,
            grid=(channels // width,),
            in_specs=[pl.BlockSpec((count, half, width), lambda i, s: (0, 0, i)), spec],
            out_specs=spec,
        ),
        out_shape=jax.ShapeDtypeStruct(base.shape, jnp.float32),
        input_output_aliases={2: 0},
        compiler_params=params(),
        cost_estimate=cost(values.size, 2 * values.size + 4 * base.size),
        name="finish",
    )(target, values, base)


def shards(
    grid_adjoint_fields,
    interp_weights,
    depart_owner,
    depart_block,
    wave_perm,
    legendre,
    mode_proj,
    mode_back,
    mode_depth,
):
    wide_count = lax.axis_size("wide")
    narrow_count = lax.axis_size("narrow")
    wide_index = lax.axis_index("wide")
    narrow_index = lax.axis_index("narrow")
    lat_dev, lon_dev, channels = grid_adjoint_fields.shape
    slot_count, lat_total, degrees = legendre.shape
    per_set = 2 * degrees // narrow_count
    blocks_per_row = lon_dev // BS
    block_count = lat_dev * blocks_per_row

    owner_band = depart_owner[:, 0]
    block_ids = jnp.arange(block_count, dtype=jnp.int32)
    capacity = (2 * block_count + wide_count - 1) // wide_count
    same_owner = owner_band[:, None] == owner_band[None, :]
    earlier = block_ids[None, :] < block_ids[:, None]
    slot_rank = jnp.sum((same_owner & earlier).astype(jnp.int32), axis=1)
    send_slot = owner_band * capacity + slot_rank
    pick_slot = jnp.arange(wide_count * capacity, dtype=jnp.int32)[:, None] == send_slot[None, :]
    source = jnp.max(jnp.where(pick_slot, block_ids[None, :], 0), axis=1)
    tables = lax.all_gather(jnp.stack([owner_band, depart_block]), "wide", axis=0, tiled=False)
    blocks = grid_adjoint_fields.reshape(block_count, BS, channels)
    contrib = jnp.einsum(
        "bai,bac->bic", interp_weights, blocks, preferred_element_type=jnp.float32
    ).astype(jnp.bfloat16)
    def packed(source, half):
        return pack(source, contrib, half).reshape(wide_count, capacity, BS // 2, channels)

    def exchange(values):
        return lax.all_to_all(values, "wide", split_axis=0, concat_axis=0, tiled=True)

    wavenumber = wave_perm.reshape(wide_count, narrow_count, slot_count)
    own_wave = lax.dynamic_index_in_dim(
        lax.dynamic_index_in_dim(wavenumber, wide_index, 0, False), narrow_index, 0, False
    )
    order = wavenumber.transpose(1, 0, 2).reshape(-1)
    trig = trig_tables(narrow_index * lon_dev, lon_dev, order)

    first_recv = exchange(packed(source, 0))
    partial = analysis(trig.T, grid_adjoint_fields, narrow_count)
    partial, tables = lax.optimization_barrier((partial, tables))
    mine = tables[:, 0] == wide_index
    rank = jnp.sum((mine[:, None, :] & earlier[None]).astype(jnp.int32), axis=2)
    rank = jnp.where(mine, rank, -1)
    arriving = rank[:, None, :] == jnp.arange(capacity, dtype=jnp.int32)[None, :, None]
    recv_targets = jnp.max(jnp.where(arriving, tables[:, 1][:, None, :], -1), axis=2).reshape(-1)
    summed = lax.psum_scatter(partial, "narrow", scatter_dimension=0, tiled=False)
    summed, first_recv, source = lax.optimization_barrier((summed, first_recv, source))
    fourier = exchange(
        summed.reshape(lat_dev, wide_count, 2 * slot_count, channels).transpose(1, 2, 0, 3)
    )
    degree_float = jnp.arange(degrees, dtype=jnp.float32)
    damping = 1.0 / (1.0 + (degree_float * (degree_float + 1.0))[:, None] * mode_depth[None, :])
    synth = modes(
        own_wave,
        legendre,
        fourier,
        mode_proj.astype(jnp.bfloat16),
        mode_back.astype(jnp.bfloat16),
        damping,
    )
    synth = exchange(synth)
    synth, second = lax.optimization_barrier((synth, packed(source, 1)))
    second_recv = exchange(second)
    rows = lax.all_gather(
        synth.reshape(per_set, lat_dev, channels).transpose(1, 0, 2), "narrow", axis=0, tiled=False
    )
    first = deposit(
        recv_targets, first_recv.reshape(wide_count * capacity, -1, channels), block_count
    )
    base = synthesis(trig, rows, first)
    out = finish(recv_targets, second_recv.reshape(wide_count * capacity, -1, channels), base)
    return out.reshape(lat_dev, lon_dev, channels)


def solution(mesh):
    in_specs = (
        P("wide", "narrow", None),
        P(("wide", "narrow"), None, None),
        P(("wide", "narrow"), None),
        P(("wide", "narrow")),
        P(),
        P(("wide", "narrow"), None, None),
        P(),
        P(),
        P(),
    )
    out_specs = P("wide", "narrow", None)
    return jax.shard_map(shards, mesh=mesh, in_specs=in_specs, out_specs=out_specs, check_vma=False)
```

```python
import math

import jax
import jax.numpy as jnp
from jax import lax
from jax.experimental import pallas as pl
from jax.experimental.pallas import tpu as pltpu
from jax.sharding import PartitionSpec as P

NLON = 2560
BS = 32
VMEM_LIMIT = 48 * 1024 * 1024
SCALE = NLON ** (-0.5)


def params():
    return pltpu.CompilerParams(vmem_limit_bytes=VMEM_LIMIT)


def cost(flops, nbytes):
    return pl.CostEstimate(flops=flops, bytes_accessed=nbytes, transcendentals=0)


def trig_tables(first_lon, lon_dev, wavenumber):
    columns = 2 * wavenumber.shape[0]
    wave = jnp.broadcast_to(wavenumber[:, None], (wavenumber.shape[0], 2)).reshape(columns)
    shift = (jnp.arange(columns, dtype=jnp.int32) % 2) * (NLON - NLON // 4)
    unit = 2.0 * math.pi / NLON
    coarse_lon = first_lon + BS * jnp.arange(lon_dev // BS, dtype=jnp.int32)
    coarse = ((coarse_lon[:, None] * wave[None, :] + shift[None, :]) % NLON).astype(jnp.float32) * unit
    fine_lon = jnp.arange(BS, dtype=jnp.int32)
    fine = ((fine_lon[:, None] * wave[None, :]) % NLON).astype(jnp.float32) * unit
    parts = lax.optimization_barrier((jnp.cos(coarse), jnp.sin(coarse), jnp.cos(fine), jnp.sin(fine)))
    cos_a, sin_a, cos_b, sin_b = parts
    table = cos_a[:, None, :] * cos_b[None, :, :] - sin_a[:, None, :] * sin_b[None, :, :]
    return table.astype(jnp.bfloat16).reshape(lon_dev, columns)


def analysis_body(trig_ref, grid_ref, out_ref):
    rows = jnp.dot(trig_ref[...], grid_ref[0], preferred_element_type=jnp.float32)
    out_ref[...] = rows.astype(jnp.bfloat16).reshape(out_ref.shape)


def analysis(trig_t, grid, sets):
    lat_dev, lon_dev, channels = grid.shape
    columns = trig_t.shape[0]
    per_set = columns // sets
    return pl.pallas_call(
        analysis_body,
        grid=(lat_dev,),
        in_specs=[
            pl.BlockSpec((columns, lon_dev), lambda a: (0, 0)),
            pl.BlockSpec((1, lon_dev, channels), lambda a: (a, 0, 0)),
        ],
        out_specs=pl.BlockSpec((sets, 1, per_set, channels), lambda a: (0, a, 0, 0)),
        out_shape=jax.ShapeDtypeStruct((sets, lat_dev, per_set, channels), jnp.bfloat16),
        compiler_params=params(),
        cost_estimate=cost(
            2 * columns * lon_dev * lat_dev * channels,
            2 * (lat_dev * (columns + lon_dev) * channels + columns * lon_dev),
        ),
        name="analysis",
    )(trig_t, grid)


def modes_body(wave_ref, legendre_ref, fourier_ref, proj_ref, back_ref, damping_ref, out_ref):
    bands, count, lat_dev, channels = fourier_ref.shape
    lats = bands * lat_dev
    slots, _, degrees = legendre_ref.shape
    first_slot = pl.program_id(0) * slots
    degree = lax.broadcasted_iota(jnp.int32, (lats, degrees), 1)
    fourier = fourier_ref[...].astype(jnp.float32)
    rows = jnp.concatenate(
        [fourier[:, q].reshape(lats, channels) for q in range(count)], axis=0
    ).astype(jnp.bfloat16)
    projected = jnp.dot(rows, proj_ref[...], preferred_element_type=jnp.float32) * SCALE
    projected = projected.astype(jnp.bfloat16)
    sums = []
    for q in range(count):
        if q % 2 == 0:
            masked = jnp.where(
                degree >= wave_ref[first_slot + q // 2],
                legendre_ref[q // 2].astype(jnp.float32),
                0.0,
            ).astype(jnp.bfloat16)
        modal = lax.dot_general(
            masked,
            projected[q * lats : (q + 1) * lats],
            (((0,), (0,)), ((), ())),
            preferred_element_type=jnp.float32,
        )
        modal = (modal * damping_ref[...]).astype(jnp.bfloat16)
        sums.append(jnp.dot(masked, modal, preferred_element_type=jnp.float32))
    back = jnp.dot(
        jnp.concatenate(sums, axis=0).astype(jnp.bfloat16),
        back_ref[...],
        preferred_element_type=jnp.float32,
    )
    for q in range(count):
        out_ref[:, q] = (
            back[q * lats : (q + 1) * lats].reshape(bands, lat_dev, channels).astype(jnp.bfloat16)
        )


def modes(wavenumber, legendre, fourier, proj, back, damping):
    slots, lats, degrees = legendre.shape
    bands, _, lat_dev, channels = fourier.shape
    group = math.gcd(slots, 4)
    spec = pl.BlockSpec((bands, 2 * group, lat_dev, channels), lambda j, w: (0, j, 0, 0))
    whole = lambda j, w: (0, 0)
    return pl.pallas_call(
        modes_body,
        grid_spec=pltpu.PrefetchScalarGridSpec(
            num_scalar_prefetch=1,
            grid=(slots // group,),
            in_specs=[
                pl.BlockSpec((group, lats, degrees), lambda j, w: (j, 0, 0)),
                spec,
                pl.BlockSpec(proj.shape, whole),
                pl.BlockSpec(back.shape, whole),
                pl.BlockSpec(damping.shape, whole),
            ],
            out_specs=spec,
        ),
        out_shape=jax.ShapeDtypeStruct(fourier.shape, jnp.bfloat16),
        compiler_params=params(),
        cost_estimate=cost(
            slots * 2 * 4 * 2 * lats * channels * degrees,
            2 * (2 * fourier.size + legendre.size) + 8 * proj.size,
        ),
        name="modes",
    )(wavenumber, legendre, fourier, proj, back, damping)


def pack_body(source_ref, contrib_ref, *refs):
    out_ref = refs[-1]

    def step(s, carry):
        out_ref[s] = contrib_ref[source_ref[s]]
        return carry

    lax.fori_loop(0, out_ref.shape[0], step, 0, unroll=4)
    if len(refs) == 2:
        table_ref = refs[0]
        per_owner = out_ref.shape[0] // table_ref.shape[0]
        for owner in range(table_ref.shape[0]):
            out_ref[(owner + 1) * per_owner - 1] = table_ref[owner]


def pack(source, contrib, half, *table):
    count = source.shape[0]
    blocks, cells, channels = contrib.shape
    shape = (count, cells // 2, channels)
    return pl.pallas_call(
        pack_body,
        grid_spec=pltpu.PrefetchScalarGridSpec(
            num_scalar_prefetch=1,
            grid=(1,),
            in_specs=[pl.BlockSpec((blocks, cells // 2, channels), lambda i, s: (0, half, 0))]
            + [pl.BlockSpec(t.shape, lambda i, s: (0, 0, 0)) for t in table],
            out_specs=pl.BlockSpec(shape, lambda i, s: (0, 0, 0)),
        ),
        out_shape=jax.ShapeDtypeStruct(shape, jnp.bfloat16),
        compiler_params=params(),
        cost_estimate=cost(math.prod(shape), 4 * math.prod(shape)),
        name="pack",
    )(source, contrib, *table)


def deposit_body(target_ref, values_ref, out_ref):
    out_ref[...] = jnp.zeros_like(out_ref)

    def step(s, carry):
        block = target_ref[s]

        @pl.when(block >= 0)
        def _():
            out_ref[block] += values_ref[s].astype(jnp.float32)

        return carry

    lax.fori_loop(0, values_ref.shape[0], step, 0, unroll=4)


def deposit(target, values, block_count):
    shape = (block_count,) + values.shape[1:]
    return pl.pallas_call(
        deposit_body,
        grid_spec=pltpu.PrefetchScalarGridSpec(
            num_scalar_prefetch=1,
            grid=(1,),
            in_specs=[pl.BlockSpec(values.shape, lambda i, s: (0, 0, 0))],
            out_specs=pl.BlockSpec(shape, lambda i, s: (0, 0, 0)),
        ),
        out_shape=jax.ShapeDtypeStruct(shape, jnp.float32),
        compiler_params=params(),
        cost_estimate=cost(values.size, 2 * values.size + 4 * math.prod(shape)),
        name="deposit",
    )(target, values)


def synthesis_body(trig_ref, rows_ref, first_ref, out_ref):
    sets, _, per_set, channels = rows_ref.shape
    half = first_ref.shape[1]
    rows = rows_ref[...].reshape(sets * per_set, channels)
    wave = jnp.dot(trig_ref[...], rows, preferred_element_type=jnp.float32) * SCALE
    wave = wave.astype(jnp.bfloat16).astype(jnp.float32).reshape(out_ref.shape)
    out_ref[:, :half] = wave[:, :half] + first_ref[...]
    out_ref[:, half:] = wave[:, half:]


def synthesis(trig, rows, first):
    sets, lat_dev, per_set, channels = rows.shape
    block_count, half, _ = first.shape
    per_row = block_count // lat_dev
    return pl.pallas_call(
        synthesis_body,
        grid=(lat_dev,),
        in_specs=[
            pl.BlockSpec(trig.shape, lambda a: (0, 0)),
            pl.BlockSpec((sets, 1, per_set, channels), lambda a: (0, a, 0, 0)),
            pl.BlockSpec((per_row, half, channels), lambda a: (a, 0, 0)),
        ],
        out_specs=pl.BlockSpec((per_row, BS, channels), lambda a: (a, 0, 0)),
        out_shape=jax.ShapeDtypeStruct((block_count, BS, channels), jnp.float32),
        compiler_params=params(),
        cost_estimate=cost(
            2 * trig.size * lat_dev * channels,
            2 * (trig.size + rows.size) + 6 * lat_dev * trig.shape[0] * channels,
        ),
        name="synthesis",
    )(trig, rows, first)


def finish_body(target_ref, values_ref, base_ref, out_ref):
    out_ref[...] = base_ref[...]

    def step(s, carry):
        block = target_ref[s]

        @pl.when(block >= 0)
        def _():
            out_ref[block] += values_ref[s].astype(jnp.float32)

        return carry

    lax.fori_loop(0, values_ref.shape[0], step, 0, unroll=4)


def finish(target, values, base):
    count, half, channels = values.shape
    block_count = base.shape[0]
    width = channels // 2
    spec = pl.BlockSpec((block_count, half, width), lambda i, s: (0, 1, i))
    return pl.pallas_call(
        finish_body,
        grid_spec=pltpu.PrefetchScalarGridSpec(
            num_scalar_prefetch=1,
            grid=(channels // width,),
            in_specs=[pl.BlockSpec((count, half, width), lambda i, s: (0, 0, i)), spec],
            out_specs=spec,
        ),
        out_shape=jax.ShapeDtypeStruct(base.shape, jnp.float32),
        input_output_aliases={2: 0},
        compiler_params=params(),
        cost_estimate=cost(values.size, 2 * values.size + 4 * base.size),
        name="finish",
    )(target, values, base)


def shards(
    grid_adjoint_fields,
    interp_weights,
    depart_owner,
    depart_block,
    wave_perm,
    legendre,
    mode_proj,
    mode_back,
    mode_depth,
):
    wide_count = lax.axis_size("wide")
    narrow_count = lax.axis_size("narrow")
    wide_index = lax.axis_index("wide")
    narrow_index = lax.axis_index("narrow")
    lat_dev, lon_dev, channels = grid_adjoint_fields.shape
    slot_count, lat_total, degrees = legendre.shape
    per_set = 2 * degrees // narrow_count
    blocks_per_row = lon_dev // BS
    block_count = lat_dev * blocks_per_row

    owner_band = depart_owner[:, 0]
    block_ids = jnp.arange(block_count, dtype=jnp.int32)
    capacity = (2 * block_count + wide_count - 1) // wide_count
    same_owner = owner_band[:, None] == owner_band[None, :]
    earlier = block_ids[None, :] < block_ids[:, None]
    slot_rank = jnp.sum((same_owner & earlier).astype(jnp.int32), axis=1)
    send_slot = owner_band * capacity + slot_rank
    pick_slot = jnp.arange(wide_count * capacity, dtype=jnp.int32)[:, None] == send_slot[None, :]
    source = jnp.max(jnp.where(pick_slot, block_ids[None, :], 0), axis=1)
    slot_target = jnp.max(jnp.where(pick_slot, depart_block[None, :], -1), axis=1).reshape(
        wide_count, capacity
    )
    table = jnp.pad(slot_target.astype(jnp.bfloat16), ((0, 0), (0, channels - capacity)))
    table = jnp.broadcast_to(table[:, None, :], (wide_count, BS // 2, channels))
    first_source = jnp.pad(source.reshape(wide_count, capacity), ((0, 0), (0, 1))).reshape(-1)
    blocks = grid_adjoint_fields.reshape(block_count, BS, channels)
    contrib = jnp.einsum(
        "bai,bac->bic", interp_weights, blocks, preferred_element_type=jnp.float32
    ).astype(jnp.bfloat16)
    def exchange(values):
        return lax.all_to_all(values, "wide", split_axis=0, concat_axis=0, tiled=True)

    wavenumber = wave_perm.reshape(wide_count, narrow_count, slot_count)
    own_wave = lax.dynamic_index_in_dim(
        lax.dynamic_index_in_dim(wavenumber, wide_index, 0, False), narrow_index, 0, False
    )
    order = wavenumber.transpose(1, 0, 2).reshape(-1)
    trig = trig_tables(narrow_index * lon_dev, lon_dev, order)

    first_recv = exchange(
        pack(first_source, contrib, 0, table).reshape(wide_count, capacity + 1, BS // 2, channels)
    )
    partial = analysis(trig.T, grid_adjoint_fields, narrow_count)
    summed = lax.psum_scatter(partial, "narrow", scatter_dimension=0, tiled=False)
    summed, first_recv, source = lax.optimization_barrier((summed, first_recv, source))
    fourier = exchange(
        summed.reshape(lat_dev, wide_count, 2 * slot_count, channels).transpose(1, 2, 0, 3)
    )
    degree_float = jnp.arange(degrees, dtype=jnp.float32)
    damping = 1.0 / (1.0 + (degree_float * (degree_float + 1.0))[:, None] * mode_depth[None, :])
    synth = modes(
        own_wave,
        legendre,
        fourier,
        mode_proj.astype(jnp.bfloat16),
        mode_back.astype(jnp.bfloat16),
        damping,
    )
    synth = exchange(synth)
    synth, second = lax.optimization_barrier((synth, pack(source, contrib, 1)))
    second_recv = exchange(second.reshape(wide_count, capacity, BS // 2, channels))
    rows = lax.all_gather(
        synth.reshape(per_set, lat_dev, channels).transpose(1, 0, 2), "narrow", axis=0, tiled=False
    )
    recv_targets = first_recv[:, capacity, 0, :capacity].astype(jnp.int32)
    first_targets = jnp.pad(recv_targets, ((0, 0), (0, 1)), constant_values=-1).reshape(-1)
    recv_targets = recv_targets.reshape(-1)
    first = deposit(
        first_targets, first_recv.reshape(first_targets.shape[0], -1, channels), block_count
    )
    base = synthesis(trig, rows, first)
    out = finish(recv_targets, second_recv.reshape(wide_count * capacity, -1, channels), base)
    return out.reshape(lat_dev, lon_dev, channels)


def solution(mesh):
    in_specs = (
        P("wide", "narrow", None),
        P(("wide", "narrow"), None, None),
        P(("wide", "narrow"), None),
        P(("wide", "narrow")),
        P(),
        P(("wide", "narrow"), None, None),
        P(),
        P(),
        P(),
    )
    out_specs = P("wide", "narrow", None)
    return jax.shard_map(shards, mesh=mesh, in_specs=in_specs, out_specs=out_specs, check_vma=False)
```

```python
import math

import jax
import jax.numpy as jnp
from jax import lax
from jax.experimental import pallas as pl
from jax.experimental.pallas import tpu as pltpu
from jax.sharding import PartitionSpec as P

NLON = 2560
BS = 32
VMEM_LIMIT = 48 * 1024 * 1024
SCALE = NLON ** (-0.5)


def params():
    return pltpu.CompilerParams(vmem_limit_bytes=VMEM_LIMIT)


def cost(flops, nbytes):
    return pl.CostEstimate(flops=flops, bytes_accessed=nbytes, transcendentals=0)


def trig_tables(first_lon, lon_dev, wavenumber):
    columns = 2 * wavenumber.shape[0]
    wave = jnp.broadcast_to(wavenumber[:, None], (wavenumber.shape[0], 2)).reshape(columns)
    shift = (jnp.arange(columns, dtype=jnp.int32) % 2) * (NLON - NLON // 4)
    unit = 2.0 * math.pi / NLON
    coarse_lon = first_lon + BS * jnp.arange(lon_dev // BS, dtype=jnp.int32)
    coarse = ((coarse_lon[:, None] * wave[None, :] + shift[None, :]) % NLON).astype(jnp.float32) * unit
    fine_lon = jnp.arange(BS, dtype=jnp.int32)
    fine = ((fine_lon[:, None] * wave[None, :]) % NLON).astype(jnp.float32) * unit
    parts = lax.optimization_barrier((jnp.cos(coarse), jnp.sin(coarse), jnp.cos(fine), jnp.sin(fine)))
    cos_a, sin_a, cos_b, sin_b = parts
    table = cos_a[:, None, :] * cos_b[None, :, :] - sin_a[:, None, :] * sin_b[None, :, :]
    return table.astype(jnp.bfloat16).reshape(lon_dev, columns)


def analysis_body(trig_ref, grid_ref, out_ref):
    rows = jnp.dot(trig_ref[...], grid_ref[0], preferred_element_type=jnp.float32)
    out_ref[...] = rows.astype(jnp.bfloat16).reshape(out_ref.shape)


def analysis(trig_t, grid, sets):
    lat_dev, lon_dev, channels = grid.shape
    columns = trig_t.shape[0]
    per_set = columns // sets
    return pl.pallas_call(
        analysis_body,
        grid=(lat_dev,),
        in_specs=[
            pl.BlockSpec((columns, lon_dev), lambda a: (0, 0)),
            pl.BlockSpec((1, lon_dev, channels), lambda a: (a, 0, 0)),
        ],
        out_specs=pl.BlockSpec((sets, 1, per_set, channels), lambda a: (0, a, 0, 0)),
        out_shape=jax.ShapeDtypeStruct((sets, lat_dev, per_set, channels), jnp.bfloat16),
        compiler_params=params(),
        cost_estimate=cost(
            2 * columns * lon_dev * lat_dev * channels,
            2 * (lat_dev * (columns + lon_dev) * channels + columns * lon_dev),
        ),
        name="analysis",
    )(trig_t, grid)


def modes_body(wave_ref, legendre_ref, fourier_ref, proj_ref, back_ref, damping_ref, out_ref):
    bands, count, lat_dev, channels = fourier_ref.shape
    lats = bands * lat_dev
    slots, _, degrees = legendre_ref.shape
    first_slot = pl.program_id(0) * slots
    degree = lax.broadcasted_iota(jnp.int32, (lats, degrees), 1)
    fourier = fourier_ref[...].astype(jnp.float32)
    rows = jnp.concatenate(
        [fourier[:, q].reshape(lats, channels) for q in range(count)], axis=0
    ).astype(jnp.bfloat16)
    projected = jnp.dot(rows, proj_ref[...], preferred_element_type=jnp.float32) * SCALE
    projected = projected.astype(jnp.bfloat16)
    sums = []
    for q in range(count):
        if q % 2 == 0:
            masked = jnp.where(
                degree >= wave_ref[first_slot + q // 2],
                legendre_ref[q // 2].astype(jnp.float32),
                0.0,
            ).astype(jnp.bfloat16)
        modal = lax.dot_general(
            masked,
            projected[q * lats : (q + 1) * lats],
            (((0,), (0,)), ((), ())),
            preferred_element_type=jnp.float32,
        )
        modal = (modal * damping_ref[...]).astype(jnp.bfloat16)
        sums.append(jnp.dot(masked, modal, preferred_element_type=jnp.float32))
    back = jnp.dot(
        jnp.concatenate(sums, axis=0).astype(jnp.bfloat16),
        back_ref[...],
        preferred_element_type=jnp.float32,
    )
    for q in range(count):
        out_ref[:, q] = (
            back[q * lats : (q + 1) * lats].reshape(bands, lat_dev, channels).astype(jnp.bfloat16)
        )


def modes(wavenumber, legendre, fourier, proj, back, damping):
    slots, lats, degrees = legendre.shape
    bands, _, lat_dev, channels = fourier.shape
    group = math.gcd(slots, 4)
    spec = pl.BlockSpec((bands, 2 * group, lat_dev, channels), lambda j, w: (0, j, 0, 0))
    whole = lambda j, w: (0, 0)
    return pl.pallas_call(
        modes_body,
        grid_spec=pltpu.PrefetchScalarGridSpec(
            num_scalar_prefetch=1,
            grid=(slots // group,),
            in_specs=[
                pl.BlockSpec((group, lats, degrees), lambda j, w: (j, 0, 0)),
                spec,
                pl.BlockSpec(proj.shape, whole),
                pl.BlockSpec(back.shape, whole),
                pl.BlockSpec(damping.shape, whole),
            ],
            out_specs=spec,
        ),
        out_shape=jax.ShapeDtypeStruct(fourier.shape, jnp.bfloat16),
        compiler_params=params(),
        cost_estimate=cost(
            slots * 2 * 4 * 2 * lats * channels * degrees,
            2 * (2 * fourier.size + legendre.size) + 8 * proj.size,
        ),
        name="modes",
    )(wavenumber, legendre, fourier, proj, back, damping)


def pack_body(source_ref, contrib_ref, *refs):
    out_ref = refs[-1]

    def step(s, carry):
        out_ref[s] = contrib_ref[source_ref[s]]
        return carry

    lax.fori_loop(0, out_ref.shape[0], step, 0, unroll=8)
    if len(refs) == 2:
        table_ref = refs[0]
        per_owner = out_ref.shape[0] // table_ref.shape[0]
        for owner in range(table_ref.shape[0]):
            out_ref[(owner + 1) * per_owner - 1] = table_ref[owner]


def pack(source, contrib, half, *table):
    count = source.shape[0]
    blocks, cells, channels = contrib.shape
    shape = (count, cells // 2, channels)
    return pl.pallas_call(
        pack_body,
        grid_spec=pltpu.PrefetchScalarGridSpec(
            num_scalar_prefetch=1,
            grid=(1,),
            in_specs=[pl.BlockSpec((blocks, cells // 2, channels), lambda i, s: (0, half, 0))]
            + [pl.BlockSpec(t.shape, lambda i, s: (0, 0, 0)) for t in table],
            out_specs=pl.BlockSpec(shape, lambda i, s: (0, 0, 0)),
        ),
        out_shape=jax.ShapeDtypeStruct(shape, jnp.bfloat16),
        compiler_params=params(),
        cost_estimate=cost(math.prod(shape), 4 * math.prod(shape)),
        name="pack",
    )(source, contrib, *table)


def deposit_body(target_ref, values_ref, out_ref):
    out_ref[...] = jnp.zeros_like(out_ref)

    def step(s, carry):
        block = target_ref[s]

        @pl.when(block >= 0)
        def _():
            out_ref[block] += values_ref[s].astype(jnp.float32)

        return carry

    lax.fori_loop(0, values_ref.shape[0], step, 0, unroll=8)


def deposit(target, values, block_count):
    shape = (block_count,) + values.shape[1:]
    return pl.pallas_call(
        deposit_body,
        grid_spec=pltpu.PrefetchScalarGridSpec(
            num_scalar_prefetch=1,
            grid=(1,),
            in_specs=[pl.BlockSpec(values.shape, lambda i, s: (0, 0, 0))],
            out_specs=pl.BlockSpec(shape, lambda i, s: (0, 0, 0)),
        ),
        out_shape=jax.ShapeDtypeStruct(shape, jnp.float32),
        compiler_params=params(),
        cost_estimate=cost(values.size, 2 * values.size + 4 * math.prod(shape)),
        name="deposit",
    )(target, values)


def synthesis_body(trig_ref, rows_ref, first_ref, out_ref):
    sets, _, per_set, channels = rows_ref.shape
    half = first_ref.shape[1]
    rows = rows_ref[...].reshape(sets * per_set, channels)
    wave = jnp.dot(trig_ref[...], rows, preferred_element_type=jnp.float32) * SCALE
    wave = wave.astype(jnp.bfloat16).astype(jnp.float32).reshape(out_ref.shape)
    out_ref[:, :half] = wave[:, :half] + first_ref[...]
    out_ref[:, half:] = wave[:, half:]


def synthesis(trig, rows, first):
    sets, lat_dev, per_set, channels = rows.shape
    block_count, half, _ = first.shape
    per_row = block_count // lat_dev
    return pl.pallas_call(
        synthesis_body,
        grid=(lat_dev,),
        in_specs=[
            pl.BlockSpec(trig.shape, lambda a: (0, 0)),
            pl.BlockSpec((sets, 1, per_set, channels), lambda a: (0, a, 0, 0)),
            pl.BlockSpec((per_row, half, channels), lambda a: (a, 0, 0)),
        ],
        out_specs=pl.BlockSpec((per_row, BS, channels), lambda a: (a, 0, 0)),
        out_shape=jax.ShapeDtypeStruct((block_count, BS, channels), jnp.float32),
        compiler_params=params(),
        cost_estimate=cost(
            2 * trig.size * lat_dev * channels,
            2 * (trig.size + rows.size) + 6 * lat_dev * trig.shape[0] * channels,
        ),
        name="synthesis",
    )(trig, rows, first)


def finish_body(target_ref, values_ref, base_ref, out_ref):
    out_ref[...] = base_ref[...]

    def step(s, carry):
        block = target_ref[s]

        @pl.when(block >= 0)
        def _():
            out_ref[block] += values_ref[s].astype(jnp.float32)

        return carry

    lax.fori_loop(0, values_ref.shape[0], step, 0, unroll=8)


def finish(target, values, base):
    count, half, channels = values.shape
    block_count = base.shape[0]
    width = channels // 2
    spec = pl.BlockSpec((block_count, half, width), lambda i, s: (0, 1, i))
    return pl.pallas_call(
        finish_body,
        grid_spec=pltpu.PrefetchScalarGridSpec(
            num_scalar_prefetch=1,
            grid=(channels // width,),
            in_specs=[pl.BlockSpec((count, half, width), lambda i, s: (0, 0, i)), spec],
            out_specs=spec,
        ),
        out_shape=jax.ShapeDtypeStruct(base.shape, jnp.float32),
        input_output_aliases={2: 0},
        compiler_params=params(),
        cost_estimate=cost(values.size, 2 * values.size + 4 * base.size),
        name="finish",
    )(target, values, base)


def shards(
    grid_adjoint_fields,
    interp_weights,
    depart_owner,
    depart_block,
    wave_perm,
    legendre,
    mode_proj,
    mode_back,
    mode_depth,
):
    wide_count = lax.axis_size("wide")
    narrow_count = lax.axis_size("narrow")
    wide_index = lax.axis_index("wide")
    narrow_index = lax.axis_index("narrow")
    lat_dev, lon_dev, channels = grid_adjoint_fields.shape
    slot_count, lat_total, degrees = legendre.shape
    per_set = 2 * degrees // narrow_count
    blocks_per_row = lon_dev // BS
    block_count = lat_dev * blocks_per_row

    owner_band = depart_owner[:, 0]
    block_ids = jnp.arange(block_count, dtype=jnp.int32)
    capacity = (2 * block_count + wide_count - 1) // wide_count
    same_owner = owner_band[:, None] == owner_band[None, :]
    earlier = block_ids[None, :] < block_ids[:, None]
    slot_rank = jnp.sum((same_owner & earlier).astype(jnp.int32), axis=1)
    send_slot = owner_band * capacity + slot_rank
    pick_slot = jnp.arange(wide_count * capacity, dtype=jnp.int32)[:, None] == send_slot[None, :]
    source = jnp.max(jnp.where(pick_slot, block_ids[None, :], 0), axis=1)
    slot_target = jnp.max(jnp.where(pick_slot, depart_block[None, :], -1), axis=1).reshape(
        wide_count, capacity
    )
    table = jnp.pad(slot_target.astype(jnp.bfloat16), ((0, 0), (0, channels - capacity)))
    table = jnp.broadcast_to(table[:, None, :], (wide_count, BS // 2, channels))
    first_source = jnp.pad(source.reshape(wide_count, capacity), ((0, 0), (0, 1))).reshape(-1)
    blocks = grid_adjoint_fields.reshape(block_count, BS, channels)
    contrib = jnp.einsum(
        "bai,bac->bic", interp_weights, blocks, preferred_element_type=jnp.float32
    ).astype(jnp.bfloat16)
    def exchange(values):
        return lax.all_to_all(values, "wide", split_axis=0, concat_axis=0, tiled=True)

    wavenumber = wave_perm.reshape(wide_count, narrow_count, slot_count)
    own_wave = lax.dynamic_index_in_dim(
        lax.dynamic_index_in_dim(wavenumber, wide_index, 0, False), narrow_index, 0, False
    )
    order = wavenumber.transpose(1, 0, 2).reshape(-1)
    trig = trig_tables(narrow_index * lon_dev, lon_dev, order)

    first_recv = exchange(
        pack(first_source, contrib, 0, table).reshape(wide_count, capacity + 1, BS // 2, channels)
    )
    partial = analysis(trig.T, grid_adjoint_fields, narrow_count)
    summed = lax.psum_scatter(partial, "narrow", scatter_dimension=0, tiled=False)
    summed, first_recv, source = lax.optimization_barrier((summed, first_recv, source))
    fourier = exchange(
        summed.reshape(lat_dev, wide_count, 2 * slot_count, channels).transpose(1, 2, 0, 3)
    )
    degree_float = jnp.arange(degrees, dtype=jnp.float32)
    damping = 1.0 / (1.0 + (degree_float * (degree_float + 1.0))[:, None] * mode_depth[None, :])
    synth = modes(
        own_wave,
        legendre,
        fourier,
        mode_proj.astype(jnp.bfloat16),
        mode_back.astype(jnp.bfloat16),
        damping,
    )
    synth = exchange(synth)
    synth, second = lax.optimization_barrier((synth, pack(source, contrib, 1)))
    second_recv = exchange(second.reshape(wide_count, capacity, BS // 2, channels))
    rows = lax.all_gather(
        synth.reshape(per_set, lat_dev, channels).transpose(1, 0, 2), "narrow", axis=0, tiled=False
    )
    recv_targets = first_recv[:, capacity, 0, :capacity].astype(jnp.int32)
    first_targets = jnp.pad(recv_targets, ((0, 0), (0, 1)), constant_values=-1).reshape(-1)
    recv_targets = recv_targets.reshape(-1)
    first = deposit(
        first_targets, first_recv.reshape(first_targets.shape[0], -1, channels), block_count
    )
    base = synthesis(trig, rows, first)
    out = finish(recv_targets, second_recv.reshape(wide_count * capacity, -1, channels), base)
    return out.reshape(lat_dev, lon_dev, channels)


def solution(mesh):
    in_specs = (
        P("wide", "narrow", None),
        P(("wide", "narrow"), None, None),
        P(("wide", "narrow"), None),
        P(("wide", "narrow")),
        P(),
        P(("wide", "narrow"), None, None),
        P(),
        P(),
        P(),
    )
    out_specs = P("wide", "narrow", None)
    return jax.shard_map(shards, mesh=mesh, in_specs=in_specs, out_specs=out_specs, check_vma=False)
```
